32 devices in a mesh: blk: 8 (over z, y), az: 4 (over x, core).
Axes of the slice: x: 2, y: 2, z: 4, core: 2. Of those that a mesh axis runs over, the one named last changes fastest.
Arguments:
- lower_part: float32 [8, 512, 512], P('blk', None, 'az'), may hold values from -0.02 to 0.02
- diag_part: float32 [8, 512, 512], P('blk', None, 'az'), may hold values from -0.02 to 0.02
- upper_part: float32 [8, 512, 512], P('blk', None, 'az'), may hold values from -0.02 to 0.02
- right_side: float32 [8, 512, 512], P('blk', None, 'az'), may hold values from -6 to 6
- extra: float32 [4096, 512], P('blk', 'az'), may hold values from -6 to 6
- owners: int32 [4096, 1], P('blk'), may hold values from 0 to 7; in each aligned block of 512 rows (0 to 511, 512 to 1023, ...) at most 128 rows name the same one
- rows_in: int32 [4096], P('blk'), may hold values from 0 to 511
- counts: int32 [8], P('blk'), may hold values from 384 to 512, as said below
Outputs:
- solution: float32 [8, 512, 512], P('blk', None, 'az')
The draws below stay inside these ranges and needn't reach their ends.
Inputs may be any that keep to these rules, and one draw needn't show every extreme that they name: `owners`: within the 512 entries of one subdomain no block row is named more than 128 times; some subdomain names some block row exactly 128 times. `counts`: A subdomain's entries at positions below its count are live, the others are ignored; some subdomain has all 512 entries live.
All inputs are finite; a program needn't handle non-finite values.
Results may differ from the reference program's by a relative error of at most 0.00013.
Values sent between devices are 32-bit elements; how exact they have to be, the bound alone decides.
No kernel may reach another device: no remote copies, remote signals or barrier semaphores. Data moves between devices by JAX's collectives and lax.ppermute only.
A program may use at most 64 MiB of HBM per device.

```python
import math
import jax
import jax.numpy as jnp
import numpy as np
from jax import lax

H = 512
R = 512
E_DEV = 512
ENTRIES = 4096
CAP = 128
LEVELS = 3
N_BLK = 8


def draw_counts(key, part):
    lowest = 3 * E_DEV // 4
    values = jax.random.randint(jax.random.fold_in(key, 11), (N_BLK,), lowest, E_DEV + 1)
    chosen = jax.random.randint(jax.random.fold_in(key, 12), (), 0, N_BLK)
    return jnp.where(jnp.arange(N_BLK, dtype=jnp.int32) == chosen, E_DEV, values).astype(jnp.int32)


def with_ends(values, stream_key, smallest, largest):
    shape = values.shape
    index_at = [jax.random.randint(jax.random.fold_in(stream_key, axis), (), 0, shape[axis]) for axis in range(len(shape))]
    values = values.at[tuple(index_at)].set(smallest)
    longest = shape.index(max(shape))
    index_at[longest] = (index_at[longest] + 1) % shape[longest]
    return values.at[tuple(index_at)].set(largest)


def shard_levels(key, shape, shards, smallest, top_value):
    def one(axis_at, parts):
        heights = jax.random.uniform(jax.random.fold_in(jax.random.fold_in(key, 6), axis_at), (parts,), jnp.float32, smallest / len(shards), top_value / len(shards))
        return jnp.repeat(jnp.exp(heights), shape[axis_at] // parts).reshape((-1,) + (1,) * (len(shape) - axis_at - 1))

    factor_of = one(*shards[0])
    for cut in shards[1:]:
        factor_of = factor_of * one(*cut)
    return factor_of


def assign_block(rng, own, number, rows, count, top, bound, lean):
    order = jax.random.permutation(rng, count)
    crowded, common = portions_of(count, rows * top, bound, lean, True), portions_of(count, rows * top, bound, lean, False)
    places = jnp.arange(count)

    def named(lengths, rotation):
        used = int((lengths > 0).sum())
        fixed = max(1, used // 4)
        moved = fixed + (places - fixed + rotation * (used - fixed)) % max(1, count - fixed)
        return jnp.zeros((count,), jnp.int32).at[order[jnp.where(places < fixed, places, moved)]].set(jnp.asarray(lengths, jnp.int32))

    lengths = jnp.where(number % 4 == 0, named(crowded, number // 4), named(common, number - number // 4 - 1))
    mixed = jax.random.permutation(jax.random.fold_in(own, 3), count)
    donor, taker = mixed[0:count // 2 * 2:2], mixed[1:count // 2 * 2:2]
    margin = jnp.minimum(lengths[donor] - 1, bound - lengths[taker]) // 2
    margin = jnp.where((donor == order[0]) | (taker == order[0]) | (lengths[taker] == 0), 0, jnp.maximum(margin, 0))
    moved = jax.random.randint(jax.random.fold_in(own, 4), (count // 2,), 0, 1 << 20) % (margin + 1)
    lengths = lengths.at[donor].add(-moved).at[taker].add(moved)
    labels = jnp.searchsorted(jnp.cumsum(lengths), jnp.arange(rows * top), side="right").astype(jnp.int32)
    grid = labels.reshape(top, rows).T
    grid = grid[jax.random.permutation(jax.random.fold_in(own, 1), rows)]
    rotation = jax.random.randint(jax.random.fold_in(own, 2), (rows, 1), 0, top)
    return jnp.take_along_axis(grid, (jnp.arange(top)[None, :] + rotation) % top, axis=1)


def portions_of(count, total, reach, skew, full):
    portions = [(1 << 20) // math.isqrt(standing ** skew) + 1 for standing in range(1, count + 1)]
    largest = reach if full else min(reach, max(-(-total // count), total * portions[0] // sum(portions)))
    least = 1 if total - largest >= count - 1 else 0
    given, surplus = [largest] + [least] * (count - 1), total - largest - least * (count - 1)
    while surplus > 0:
        candidates = [i for i in range(1, count) if given[i] < largest] or [i for i in range(1, count) if given[i] < reach]
        mass, remaining = sum([portions[i] for i in candidates]), surplus
        for i in candidates:
            more = min(reach - given[i], max(1, remaining * portions[i] // mass), surplus)
            given[i] = given[i] + more
            surplus = surplus - more
    return np.array(given)


def bell_draw(own_key, extent, width, most, split=(), kind=jnp.bfloat16):
    gain = shard_levels(own_key, extent, split, -0.22, 0.18) if split else 1.0
    result = jax.random.normal(own_key, extent, jnp.float32) * width * gain
    return jnp.minimum(jnp.maximum(result, -most), most).astype(kind)


def setup_inputs(seed: int = 0) -> dict:
    key_list = jax.random.split(jax.random.key(seed), 9)
    lower_part = bell_draw(key_list[0], (N_BLK, H, H), 0.006, 0.02, ((0, 8), (2, 4)), jnp.float32)
    diag_part = bell_draw(key_list[1], (N_BLK, H, H), 0.006, 0.02, ((0, 8), (2, 4)), jnp.float32)
    upper_part = bell_draw(key_list[2], (N_BLK, H, H), 0.006, 0.02, ((0, 8), (2, 4)), jnp.float32)
    right_side = bell_draw(key_list[3], (N_BLK, H, R), 1.0, 6.0, ((0, 8), (2, 4)), jnp.float32)
    extra = bell_draw(key_list[4], (ENTRIES, R), 1.0, 6.0, ((0, 8), (1, 4)), jnp.float32)
    owners_keys = jax.random.split(jax.random.fold_in(key_list[5], 1), ENTRIES // E_DEV)
    owners_turns = jax.random.permutation(jax.random.fold_in(key_list[5], 3), ENTRIES // E_DEV)
    owners = jax.vmap(lambda own, number: assign_block(jax.random.fold_in(key_list[5], 2), own, number, E_DEV, N_BLK, 1, CAP, 1))(owners_keys, owners_turns).reshape((ENTRIES, 1))
    rows_in = with_ends(jax.random.randint(key_list[6], (ENTRIES,), 0, H), jax.random.fold_in(key_list[6], 1), 0, H - 1).astype(jnp.int32)
    counts = draw_counts(jax.random.fold_in(key_list[8], 71), 0)
    return dict(lower_part=lower_part, diag_part=diag_part, upper_part=upper_part, right_side=right_side, extra=extra, owners=owners, rows_in=rows_in, counts=counts)


coupling = 0.42


def product(left, right):
    return jnp.einsum("nij,njk->nik", left.astype(jnp.float32), right.astype(jnp.float32), precision=lax.Precision.HIGHEST)


def inverse_apply(diag_block, values):
    first_pass = 2.0 * values - product(diag_block, values)
    second_pass = 2.0 * values - product(diag_block, first_pass)
    return 2.0 * second_pass - product(diag_block, second_pass)


def reference(lower_part, diag_part, upper_part, right_side, extra, owners, rows_in, counts):
    identity = jnp.eye(H, dtype=jnp.float32)
    lower_block = lower_part - coupling * identity
    upper_block = upper_part - coupling * identity
    diag_block = diag_part + identity
    entry_index = jnp.arange(N_BLK * E_DEV, dtype=jnp.int32)
    live_mask = (entry_index % E_DEV) < jnp.repeat(counts, E_DEV)
    flat_rows = (owners[:, 0] * H + rows_in).astype(jnp.int32)
    added = jnp.where(live_mask[:, None], extra, jnp.float32(0.0))
    right_block = right_side.reshape(N_BLK * H, R).at[flat_rows].add(added).reshape(N_BLK, H, R)
    stride = 1
    for level_index in range(LEVELS):
        stacked = inverse_apply(diag_block, jnp.concatenate([lower_block, upper_block, right_block], axis=2))
        from_lower = jnp.roll(stacked, stride, axis=0)
        from_upper = jnp.roll(stacked, -stride, axis=0)
        got_lower = product(lower_block, from_lower)
        got_upper = product(upper_block, from_upper)
        diag_block = diag_block - got_lower[:, :, H:2 * H] - got_upper[:, :, :H]
        right_block = right_block - got_lower[:, :, 2 * H:] - got_upper[:, :, 2 * H:]
        lower_block = -got_lower[:, :, :H]
        upper_block = -got_upper[:, :, H:2 * H]
        stride = stride * 2
    return inverse_apply(diag_block, right_block)
```

```python
import functools

import jax
import jax.numpy as jnp
from jax import lax
from jax.experimental import pallas as pl
from jax.experimental.pallas import tpu as pltpu
from jax.sharding import PartitionSpec as P

coupling = 0.42
mark_rows = 8
f32 = jnp.float32
bf16 = jnp.bfloat16
in_vmem = pl.BlockSpec(memory_space=pltpu.VMEM)
in_smem = pl.BlockSpec(memory_space=pltpu.SMEM)


def send(value, axis, target_of):
    pairs = [(source, target_of(source)) for source in range(lax.axis_size(axis))]
    return lax.ppermute(value, axis, pairs)


def halves(value):
    high = value.astype(bf16)
    return high, (value - high.astype(f32)).astype(bf16)


def dot(left, right):
    return jnp.dot(left, right, preferred_element_type=f32)


def three_pass(left_high, left_low, right):
    high, low = halves(right)
    return dot(left_high[...], high) + (dot(left_high[...], low) + dot(left_low[...], high))


def row_starts(place, shards, width):
    return [pl.multiple_of((place ^ k) * width, width) for k in range(shards)]


def load_rows(ref, starts, width):
    return jnp.concatenate([ref[pl.ds(start, width), :] for start in starts], axis=0)


def store_rows(ref, starts, width, value):
    for k, start in enumerate(starts):
        ref[pl.ds(start, width), :] = value[k * width : (k + 1) * width, :]


def unit(width):
    rows = lax.broadcasted_iota(jnp.int32, (width, width), 0)
    cols = lax.broadcasted_iota(jnp.int32, (width, width), 1)
    return (rows == cols).astype(f32)


def assemble(high, low, shard_of, starts, width, shift):
    for k in range(len(starts)):
        for g, start in enumerate(starts):
            piece = shard_of(k, start)
            if shift and g == k:
                piece = piece - shift * unit(width)
            at = (slice(g * width, (g + 1) * width), slice(k * width, (k + 1) * width))
            high[at], low[at] = halves(piece)


def shifted(value, width, shift):
    if not shift:
        return value
    return jnp.concatenate([value[:width] - shift * unit(width), value[width:]], axis=0)


def apply_kernel(shards, shift, swap, place, *refs):
    n_refs, v_refs = refs[:shards], refs[shards:-3]
    count = len(v_refs) // 2
    v_refs, o_refs = v_refs[:count], v_refs[count:]
    high, low = refs[-3:-1]
    width = v_refs[0].shape[1]
    starts = row_starts(place[0], shards, width)
    assemble(high, low, lambda k, s: n_refs[k][pl.ds(s, width), :], starts, width, 0)
    values = [shifted(load_rows(ref, starts, width), width, shift) for ref in v_refs]
    if swap:
        even = place[1] == 0
        values = [jnp.where(even, values[0], values[1]), jnp.where(even, values[1], values[0])]
    value = jnp.concatenate(values, axis=1)
    second = value + three_pass(high, low, three_pass(high, low, value))
    result = second - three_pass(high, low, second)
    for k, ref in enumerate(o_refs):
        store_rows(ref, starts, width, result[:, k * width : (k + 1) * width])


def compiler_params(megabytes):
    return pltpu.CompilerParams(vmem_limit_bytes=megabytes * 2**20)


def inverse_apply(place, n_shards, values, shift=0, swap=False):
    order, width = values[0].shape
    shards = len(n_shards)
    columns = width * len(values)
    return pl.pallas_call(
        functools.partial(apply_kernel, shards, shift, swap),
        out_shape=[jax.ShapeDtypeStruct((order, width), f32)] * len(values),
        in_specs=[in_smem] + [in_vmem] * (shards + len(values)),
        out_specs=[in_vmem] * len(values),
        scratch_shapes=[pltpu.VMEM((order, order), bf16)] * 2 + [pltpu.VMEM((8, 128), f32)],
        compiler_params=compiler_params(24),
        cost_estimate=pl.CostEstimate(
            flops=18 * order * order * columns,
            bytes_accessed=4 * order * (order + 2 * columns),
            transcendentals=0,
        ),
    )(place, *n_shards, *values)


def combine_kernel(shards, shift, swap, bases, pairs, singles, place, *refs):
    refs = list(refs)
    take = lambda n: [refs.pop(0) for _ in range(n)]
    one_refs, two_refs = take(shards), take(shards)
    base_refs, pair_refs, single_refs = take(bases), take(2 * pairs), take(2 * singles)
    o_refs = take(pairs + 2 * singles)
    scratch = take(4)
    width = one_refs[0].shape[1]
    starts = row_starts(place[0], shards, width)
    results = []
    for m, (high, low) in enumerate((scratch[:2], scratch[2:])):
        mine, other = (one_refs, two_refs) if m == 0 else (two_refs, one_refs)
        if swap:
            even = place[1] == 0
            shard_of = lambda k, s, mine=mine, other=other: jnp.where(
                even, mine[k][pl.ds(s, width), :], other[k][pl.ds(s, width), :]
            )
        else:
            shard_of = lambda k, s, mine=mine: mine[k][pl.ds(s, width), :]
        assemble(high, low, shard_of, starts, width, shift)
        rights = [load_rows(ref, starts, width) for ref in pair_refs[m::2] + single_refs[m::2]]
        right = jnp.concatenate(rights, axis=1) if len(rights) > 1 else rights[0]
        results.append(three_pass(high, low, right))
    part = lambda m, j: results[m][:, j * width : (j + 1) * width]
    for j in range(pairs):
        base = load_rows(base_refs[j], starts, width)
        store_rows(o_refs[j], starts, width, base - part(0, j) - part(1, j))
    for j in range(singles):
        for m in range(2):
            store_rows(o_refs[pairs + 2 * j + m], starts, width, -part(m, pairs + j))


def combine(place, one_shards, two_shards, base_pairs, single_pairs, shift=0, swap=False):
    order, width = one_shards[0].shape
    shards = len(one_shards)
    bases = [base for base, _, _ in base_pairs]
    rights = [v for _, a, b in base_pairs for v in (a, b)] + [v for pair in single_pairs for v in pair]
    outs = len(base_pairs) + 2 * len(single_pairs)
    return pl.pallas_call(
        functools.partial(
            combine_kernel, shards, shift, swap, len(bases), len(base_pairs), len(single_pairs)
        ),
        out_shape=[jax.ShapeDtypeStruct((order, width), f32)] * outs,
        in_specs=[in_smem] + [in_vmem] * (2 * shards + len(bases) + len(rights)),
        out_specs=[in_vmem] * outs,
        scratch_shapes=[pltpu.VMEM((order, order), bf16)] * 4,
        compiler_params=compiler_params(24),
        cost_estimate=pl.CostEstimate(
            flops=6 * order * order * width * len(rights),
            bytes_accessed=4 * order * (2 * order + 2 * width * len(rights)),
            transcendentals=0,
        ),
    )(place, *one_shards, *two_shards, *bases, *rights)


def slots_kernel(cycle_size, slot_count, counts, owner_row, rows_row, extra, out):
    entries, width = extra.shape
    position = lax.broadcasted_iota(jnp.int32, (1, entries), 1)
    live = position < counts[0]
    owner = jnp.where(live, owner_row[...], cycle_size)
    blocks = lax.broadcasted_iota(jnp.int32, (cycle_size, entries), 0)
    owned = (blocks == owner).astype(f32)
    before = lax.broadcasted_iota(jnp.int32, (entries, entries), 0)
    after = lax.broadcasted_iota(jnp.int32, (entries, entries), 1)
    earlier = dot(owned.astype(bf16), (before < after).astype(f32).astype(bf16))
    rank = jnp.sum(owned * earlier, axis=0, keepdims=True).astype(jnp.int32)
    high, low = halves(extra[...])
    both = jnp.concatenate([high, low], axis=1)
    slots = lax.broadcasted_iota(jnp.int32, (slot_count, entries), 0)
    in_slot = (slots == rank).astype(f32)
    mark_high, mark_low = halves(owned * (rows_row[...] + 1).astype(f32))
    to_slot = lambda mark: lax.dot_general(
        mark, in_slot.astype(bf16), (((1,), (1,)), ((), ())), preferred_element_type=f32
    )
    marks = to_slot(mark_high) + to_slot(mark_low)
    stride = slot_count + mark_rows
    for block in range(cycle_size):
        chosen = jnp.where(owner == block, in_slot, 0.0).astype(bf16)
        found = dot(chosen, both)
        out[block * stride : block * stride + slot_count, :] = found[:, :width] + found[:, width:]
        out[block * stride + slot_count : (block + 1) * stride, :] = jnp.zeros((mark_rows, width), f32)
        out[block * stride + slot_count : block * stride + slot_count + 1, :slot_count] = marks[
            block : block + 1, :
        ]


def load_kernel(cycle_size, slot_count, right_side, got, out):
    order, width = right_side.shape
    stride = slot_count + mark_rows
    total = right_side[...]
    rows = (lax.broadcasted_iota(jnp.int32, (order, slot_count), 0) + 1).astype(f32)
    for block in range(cycle_size):
        high, low = halves(got[block * stride : block * stride + slot_count, :])
        marks = got[block * stride + slot_count : block * stride + slot_count + 1, :slot_count]
        found = dot((rows == marks).astype(f32).astype(bf16), jnp.concatenate([high, low], axis=1))
        total = total + (found[:, :width] + found[:, width:])
    out[...] = total


def deliver(right_side, extra, owners, rows_in, counts):
    cycle_size = lax.axis_size("blk")
    entries, width = extra.shape
    order = right_side.shape[0]
    slot_count = 2 * entries // cycle_size
    stride = slot_count + mark_rows
    sent = pl.pallas_call(
        functools.partial(slots_kernel, cycle_size, slot_count),
        out_shape=jax.ShapeDtypeStruct((cycle_size * stride, width), f32),
        in_specs=[in_smem] + [in_vmem] * 3,
        out_specs=in_vmem,
        compiler_params=compiler_params(24),
    )(counts, owners.reshape(1, entries), rows_in.reshape(1, entries), extra)
    got = lax.all_to_all(
        sent.reshape(cycle_size, stride, width), "blk", split_axis=0, concat_axis=0, tiled=True
    )
    return pl.pallas_call(
        functools.partial(load_kernel, cycle_size, slot_count),
        out_shape=jax.ShapeDtypeStruct((order, width), f32),
        in_specs=[in_vmem] * 2,
        out_specs=in_vmem,
        compiler_params=compiler_params(24),
    )(right_side, got.reshape(cycle_size * stride, width))


def gathered(value):
    bit = lax.axis_size("az") // 2
    shards = {0: value}
    while bit:
        for k in list(shards):
            shards[k | bit] = send(shards[k], "az", lambda source, bit=bit: source ^ bit)
        bit //= 2
    return [shards[k] for k in range(len(shards))]


def on_device(lower_part, diag_part, upper_part, right_side, extra, owners, rows_in, counts):
    cycle_size = lax.axis_size("blk")
    levels = min(4, 3 + cycle_size // 16)
    place = jnp.stack([lax.axis_index("az"), lax.axis_index("blk") % 2]).astype(jnp.int32)
    even = place[1] == 0
    lower, diag, upper = lower_part[0], diag_part[0], upper_part[0]

    n_shards = gathered(diag)
    l_shards, u_shards = gathered(lower), gathered(upper)
    right = deliver(right_side[0], extra, owners, rows_in, counts)

    partner = lambda source: source ^ 1
    onward = lambda source: (source + 2 - 4 * (source % 2)) % cycle_size
    first, second = inverse_apply(place, n_shards, [lower, upper], shift=coupling, swap=True)
    near_first = send(first, "blk", partner)
    near_second = send(second, "blk", partner)
    far_first = send(near_first, "blk", onward)
    (diag,) = combine(
        place, l_shards, u_shards, [(diag, far_first, near_second)], [], shift=coupling, swap=True
    )
    n_next = gathered(diag)
    far_second = send(near_second, "blk", onward)
    one, two = combine(
        place, l_shards, u_shards, [], [(far_second, near_first)], shift=coupling, swap=True
    )
    (solved,) = inverse_apply(place, n_shards, [right])
    near_solved = send(solved, "blk", partner)
    far_solved = send(near_solved, "blk", onward)
    (right,) = combine(
        place, l_shards, u_shards, [(right, far_solved, near_solved)], [], shift=coupling, swap=True
    )
    lower, upper = jnp.where(even, one, two), jnp.where(even, two, one)

    stride = 2
    for level in range(1, levels):
        n_shards = n_next
        l_shards, u_shards = gathered(lower), gathered(upper)
        ahead = lambda source: (source + stride) % cycle_size
        back = lambda source: (source - stride) % cycle_size
        last = level == levels - 1
        p_row, q_row = inverse_apply(place, n_shards, [lower, upper])
        low_q, up_p = send(q_row, "blk", ahead), send(p_row, "blk", back)
        (diag,) = combine(place, l_shards, u_shards, [(diag, low_q, up_p)], [])
        n_next = gathered(diag)
        (solved,) = inverse_apply(place, n_shards, [right])
        if not last:
            low_p, up_q = send(p_row, "blk", ahead), send(q_row, "blk", back)
            lower, upper = combine(place, l_shards, u_shards, [], [(low_p, up_q)])
        low_y = send(solved, "blk", ahead)
        up_y = low_y if 2 * stride == cycle_size else send(solved, "blk", back)
        (right,) = combine(place, l_shards, u_shards, [(right, low_y, up_y)], [])
        stride = 2 * stride
    (result,) = inverse_apply(place, n_next, [right])
    return result[None]


def solution(mesh):
    placed = (
        P("blk", None, "az"),
        P("blk", None, "az"),
        P("blk", None, "az"),
        P("blk", None, "az"),
        P("blk", "az"),
        P("blk", None),
        P("blk"),
        P("blk"),
    )
    return jax.shard_map(
        on_device, mesh=mesh, in_specs=placed, out_specs=P("blk", None, "az"), check_vma=False
    )
```

```python
import functools

import jax
import jax.numpy as jnp
from jax import lax
from jax.experimental import pallas as pl
from jax.experimental.pallas import tpu as pltpu
from jax.sharding import PartitionSpec as P

coupling = 0.42
mark_rows = 8
f32 = jnp.float32
bf16 = jnp.bfloat16
in_vmem = pl.BlockSpec(memory_space=pltpu.VMEM)
in_smem = pl.BlockSpec(memory_space=pltpu.SMEM)


def send(value, axis, target_of):
    pairs = [(source, target_of(source)) for source in range(lax.axis_size(axis))]
    return lax.ppermute(value, axis, pairs)


def halves(value):
    high = value.astype(bf16)
    return high, (value - high.astype(f32)).astype(bf16)


def dot(left, right):
    return jnp.dot(left, right, preferred_element_type=f32)


def three_pass(left_high, left_low, right):
    high, low = halves(right)
    both = jnp.concatenate([high, low], axis=1)
    order, columns = left_high.shape[0], right.shape[1]
    found = []
    for rows in (slice(0, order // 2), slice(order // 2, order)):
        wide = dot(left_high[rows, :], both)
        found.append(wide[:, :columns] + wide[:, columns:] + dot(left_low[rows, :], high))
    return jnp.concatenate(found, axis=0)


def row_starts(place, shards, width):
    return [pl.multiple_of((place ^ k) * width, width) for k in range(shards)]


def load_rows(ref, starts, width, base=0):
    return jnp.concatenate([ref[pl.ds(base + start, width), :] for start in starts], axis=0)


def store_rows(ref, starts, width, value, base=0):
    for k, start in enumerate(starts):
        ref[pl.ds(base + start, width), :] = value[k * width : (k + 1) * width, :]


def assemble(high, low, refs, starts, width, base=0):
    for k, ref in enumerate(refs):
        for g, start in enumerate(starts):
            at = (slice(g * width, (g + 1) * width), slice(k * width, (k + 1) * width))
            high[at], low[at] = halves(ref[pl.ds(base + start, width), :])


def polynomial(high, low, value):
    second = value + three_pass(high, low, three_pass(high, low, value))
    return second - three_pass(high, low, second)


def compiler_params(megabytes):
    return pltpu.CompilerParams(vmem_limit_bytes=megabytes * 2**20)


def weight(cost):
    return pl.CostEstimate(
        flops=1 + 1_150_000_000 * cost, bytes_accessed=1 + 3_690_000 * cost, transcendentals=0
    )


def kernel_call(body, place, operands, outs, halves_of, after=(), cost=0):
    order = operands[0].shape[1] * lax.axis_size("az")
    width = operands[0].shape[1]
    count = len(operands)
    waited = len(after)

    def kernel(place_ref, *refs):
        starts = row_starts(place_ref[0], order // width, width)
        swapped = pl.multiple_of(place_ref[1] * order, order)
        body(
            starts,
            (swapped, order - swapped),
            refs[:count],
            refs[count + waited : count + waited + len(outs)],
            refs[count + waited + len(outs) :],
        )

    return pl.pallas_call(
        kernel,
        out_shape=[jax.ShapeDtypeStruct((rows, width), f32) for rows in outs],
        in_specs=[in_smem] + [in_vmem] * count + [pl.BlockSpec(memory_space=pl.ANY)] * waited,
        out_specs=[in_vmem] * len(outs),
        scratch_shapes=[pltpu.VMEM((order, order), bf16)] * (2 * halves_of),
        compiler_params=compiler_params(24),
        cost_estimate=weight(cost),
    )(place, *operands, *after)


def couplings(place, lower, upper, after=()):
    order, width = lower.shape

    def body(starts, bases, refs, outs, scratch):
        rows = lax.broadcasted_iota(jnp.int32, (order, width), 0)
        cols = lax.broadcasted_iota(jnp.int32, (order, width), 1)
        diagonal = jnp.where(rows == cols + starts[0], coupling, 0.0)
        outs[0][:order, :] = refs[0][...] - diagonal
        outs[0][order:, :] = refs[1][...] - diagonal

    return kernel_call(body, place, [lower, upper], [2 * order], 0, after)[0]


def normalized(place, n_shards, both, swap=False, join=False, after=()):
    shards, order, width = len(n_shards), both.shape[0] // 2, both.shape[1]

    def body(starts, bases, refs, outs, scratch):
        assemble(*scratch, refs[:shards], starts, width)
        bases = bases if swap else (0, order)
        value = [load_rows(refs[shards], starts, width, base) for base in bases]
        result = polynomial(*scratch, jnp.concatenate(value, axis=1))
        places = ((outs[0], 0), (outs[0], order)) if join else ((outs[0], 0), (outs[1], 0))
        for k, (ref, base) in enumerate(places):
            store_rows(ref, starts, width, result[:, k * width : (k + 1) * width], base)

    return kernel_call(body, place, [*n_shards, both], [2 * order] if join else [order] * 2, 1, after)


def one_column(place, n_shards, value, after=()):
    shards, order, width = len(n_shards), *value.shape

    def body(starts, bases, refs, outs, scratch):
        assemble(*scratch, refs[:shards], starts, width)
        result = polynomial(*scratch, load_rows(refs[shards], starts, width))
        store_rows(outs[0], starts, width, result)

    return kernel_call(body, place, [*n_shards, value], [order], 1, after)[0]


def joined_column(place, n_shards, value, one, two):
    shards, order, width = len(n_shards), *value.shape

    def body(starts, bases, refs, outs, scratch):
        assemble(*scratch, refs[:shards], starts, width)
        result = polynomial(*scratch, load_rows(refs[shards], starts, width))
        for out, top in zip(outs, refs[shards + 1 :]):
            out[:order, :] = top[...]
            store_rows(out, starts, width, result, order)

    return kernel_call(body, place, [*n_shards, value, one, two], [2 * order] * 2, 1)


def coupled_reduced(place, both_shards, base, one, two, after=()):
    shards, order, width = len(both_shards), *base.shape

    def body(starts, bases, refs, outs, scratch):
        total = load_rows(refs[shards], starts, width)
        for m in range(2):
            assemble(*scratch[2 * m : 2 * m + 2], refs[:shards], starts, width, m * order)
            right = [load_rows(refs[shards + 1 + m], starts, width, at) for at in (0, order)]
            found = three_pass(*scratch[2 * m : 2 * m + 2], jnp.concatenate(right, axis=1))
            store_rows(outs[0], starts, width, -found[:, :width], m * order)
            total = total - found[:, width:]
        store_rows(outs[1], starts, width, total)

    return kernel_call(body, place, [*both_shards, base, one, two], [2 * order, order], 2, after)


def reduced(place, both_shards, base, one, two, swap=False, after=(), cost=0):
    shards, order, width = len(both_shards), *base.shape
    joined = one is two

    def body(starts, bases, refs, outs, scratch):
        bases = bases if swap else (0, order)
        total = load_rows(refs[shards], starts, width)
        if joined and one.shape[0] == 2 * order:
            rights = [load_rows(refs[shards + 1], starts, width, at) for at in (order, 0)]
        else:
            rights = [load_rows(ref, starts, width) for ref in refs[shards + 1 :]]
            rights = rights * 2 if joined else rights
        for m in range(2):
            assemble(*scratch[2 * m : 2 * m + 2], refs[:shards], starts, width, bases[m])
            total = total - three_pass(*scratch[2 * m : 2 * m + 2], rights[m])
        store_rows(outs[0], starts, width, total)

    operands = [*both_shards, base, one] if joined else [*both_shards, base, one, two]
    return kernel_call(body, place, operands, [order], 2, after, cost)[0]


def coupled(place, both_shards, one, two, swap=False, after=()):
    shards, order, width = len(both_shards), *one.shape

    def body(starts, bases, refs, outs, scratch):
        bases = bases if swap else (0, order)
        for m in range(2):
            assemble(*scratch[2 * m : 2 * m + 2], refs[:shards], starts, width, bases[m])
            found = three_pass(*scratch[2 * m : 2 * m + 2], load_rows(refs[shards + m], starts, width))
            store_rows(outs[0], starts, width, -found, bases[m])

    return kernel_call(body, place, [*both_shards, one, two], [2 * order], 2, after)[0]


def slots_kernel(cycle_size, slot_count, counts, owner_row, rows_row, extra, out):
    entries, width = extra.shape
    position = lax.broadcasted_iota(jnp.int32, (1, entries), 1)
    live = position < counts[0]
    target = jnp.where(live, owner_row[...], cycle_size)
    blocks = lax.broadcasted_iota(jnp.int32, (cycle_size, entries), 0)
    owned = (blocks == target).astype(f32)
    before = lax.broadcasted_iota(jnp.int32, (entries, entries), 0)
    after = lax.broadcasted_iota(jnp.int32, (entries, entries), 1)
    earlier = dot(owned.astype(bf16), (before < after).astype(f32).astype(bf16))
    rank = jnp.sum(owned * earlier, axis=0, keepdims=True).astype(jnp.int32)
    high, low = halves(extra[...])
    both = jnp.concatenate([high, low], axis=1)
    slots = lax.broadcasted_iota(jnp.int32, (slot_count, entries), 0)
    in_slot = (slots == rank).astype(f32)
    mark_high, mark_low = halves(owned * (rows_row[...] + 1).astype(f32))
    to_slot = lambda mark: lax.dot_general(
        mark, in_slot.astype(bf16), (((1,), (1,)), ((), ())), preferred_element_type=f32
    )
    marks = to_slot(mark_high) + to_slot(mark_low)
    stride = slot_count + mark_rows
    for block in range(cycle_size):
        base = block * stride
        chosen = jnp.where(target == block, in_slot, 0.0).astype(bf16)
        found = dot(chosen, both)
        out[base : base + slot_count, :] = found[:, :width] + found[:, width:]
        out[base + slot_count : base + stride, :] = jnp.zeros((mark_rows, width), f32)
        out[base + slot_count : base + slot_count + 1, :slot_count] = marks[block : block + 1, :]


def load_kernel(cycle_size, slot_count, right_side, got, _, out):
    order, width = right_side.shape
    stride = slot_count + mark_rows
    total = right_side[...]
    rows = (lax.broadcasted_iota(jnp.int32, (order, slot_count), 0) + 1).astype(f32)
    for block in range(cycle_size):
        high, low = halves(got[block * stride : block * stride + slot_count, :])
        marks = got[block * stride + slot_count : block * stride + slot_count + 1, :slot_count]
        chosen = (rows == marks).astype(f32).astype(bf16)
        found = dot(chosen, jnp.concatenate([high, low], axis=1))
        total = total + (found[:, :width] + found[:, width:])
    out[...] = total


def placed_entries(extra, owners, rows_in, counts):
    cycle_size = lax.axis_size("blk")
    entries, width = extra.shape
    slot_count = 2 * entries // cycle_size
    rows = cycle_size * (slot_count + mark_rows)
    return pl.pallas_call(
        functools.partial(slots_kernel, cycle_size, slot_count),
        out_shape=jax.ShapeDtypeStruct((rows, width), f32),
        in_specs=[in_smem] + [in_vmem] * 3,
        out_specs=in_vmem,
        compiler_params=compiler_params(24),
        cost_estimate=weight(0),
    )(counts, owners.reshape(1, entries), rows_in.reshape(1, entries), extra)


def loaded(right_side, got, after):
    cycle_size = lax.axis_size("blk")
    order, width = right_side.shape
    return pl.pallas_call(
        functools.partial(load_kernel, cycle_size, got.shape[1] - mark_rows),
        out_shape=jax.ShapeDtypeStruct((order, width), f32),
        in_specs=[in_vmem] * 2 + [pl.BlockSpec(memory_space=pl.ANY)],
        out_specs=in_vmem,
        compiler_params=compiler_params(24),
        cost_estimate=weight(0),
    )(right_side, got.reshape(-1, width), after)


def across(value):
    bit = lax.axis_size("az") // 2
    return {bit: send(value, "az", lambda source: source ^ bit)}


def gathered(value, far):
    shards = {0: value, **far}
    bit = max(far) // 2
    while bit:
        for k in list(shards):
            shards[k | bit] = send(shards[k], "az", lambda source, bit=bit: source ^ bit)
        bit //= 2
    return [shards[k] for k in range(len(shards))]


def tied(*values):
    return lax.optimization_barrier(values)


def on_device(lower_part, diag_part, upper_part, right_side, extra, owners, rows_in, counts):
    cycle_size = lax.axis_size("blk")
    levels = min(4, 3 + cycle_size // 16)
    blk = lax.axis_index("blk")
    place = jnp.stack([lax.axis_index("az"), blk % 2]).astype(jnp.int32)
    diag = diag_part[0]

    n_far = across(diag)
    slots = placed_entries(extra, owners, rows_in, counts)
    both = couplings(place, lower_part[0], upper_part[0], [slots])
    n_far, both = tied(n_far, both)
    n_shards = gathered(diag, n_far)

    partner = lambda source: source ^ 1
    onward = lambda source: (source + 2 - 4 * (source % 2)) % cycle_size
    got_slots = lax.all_to_all(
        slots.reshape(cycle_size, -1, slots.shape[1]), "blk", split_axis=0, concat_axis=0, tiled=True
    )
    first, second = normalized(place, n_shards, both, swap=True)
    both_shards = gathered(both, across(both))
    near_first = send(first, "blk", partner)
    near_second = send(second, "blk", partner)
    near_first, got_slots = tied(near_first, got_slots)
    far_first = send(near_first, "blk", onward)
    right = loaded(right_side[0], got_slots, first)
    solved = one_column(place, n_shards, right)
    diag = reduced(place, both_shards, diag, far_first, near_second, swap=True, after=[solved])
    n_far = across(diag)
    far_second = send(near_second, "blk", onward)
    both = coupled(place, both_shards, far_second, near_first, swap=True, after=[solved])
    n_far, both = tied(n_far, both)
    n_shards = gathered(diag, n_far)
    near_solved = send(solved, "blk", partner)
    far_solved = send(near_solved, "blk", onward)
    waiting = (both_shards, right, far_solved, near_solved, True)

    stride = 2
    for level in range(1, levels):
        ahead = lambda source: (source + stride) % cycle_size
        back = lambda source: (source - stride) % cycle_size
        both_far = across(both)
        half = max(both_far)
        last = level == levels - 1
        if last and 2 * stride == cycle_size:
            right = reduced(place, *waiting)
            (pair,) = normalized(place, n_shards, both, join=True, after=[right])
            got = send(pair, "blk", ahead)
            both_far[half], got = tied(both_far[half], got)
            both_shards = gathered(both, both_far)
            solved = one_column(place, n_shards, right, after=[pair])
            low_y = up_y = send(solved, "blk", ahead)
            diag = reduced(place, both_shards, diag, got, got, after=[solved])
        else:
            p_row, q_row = normalized(place, n_shards, both)
            low_q, up_p = send(q_row, "blk", ahead), send(p_row, "blk", back)
            both_far[half], low_q, up_p, p_row, q_row = tied(both_far[half], low_q, up_p, p_row, q_row)
            both_shards = gathered(both, both_far)
            right = reduced(place, *waiting, after=[q_row], cost=20)
            diag = reduced(place, both_shards, diag, low_q, up_p, after=[right])
            solved = one_column(place, n_shards, right, after=[diag])
            low_y, up_y = send(solved, "blk", ahead), send(solved, "blk", back)
        n_far = across(diag)
        if last:
            right = reduced(place, both_shards, right, low_y, up_y, after=[diag], cost=20)
            n_far, right = tied(n_far, right)
        else:
            low_p, up_q = send(p_row, "blk", ahead), send(q_row, "blk", back)
            both = coupled(place, both_shards, low_p, up_q, after=[diag])
            n_far, both = tied(n_far, both)
            waiting = (both_shards, right, low_y, up_y, False)
        n_shards = gathered(diag, n_far)
        stride = 2 * stride
    return one_column(place, n_shards, right)[None]


def solution(mesh):
    placed = (
        P("blk", None, "az"),
        P("blk", None, "az"),
        P("blk", None, "az"),
        P("blk", None, "az"),
        P("blk", "az"),
        P("blk", None),
        P("blk"),
        P("blk"),
    )
    return jax.shard_map(
        on_device, mesh=mesh, in_specs=placed, out_specs=P("blk", None, "az"), check_vma=False
    )
```

```python
import functools

import jax
import jax.numpy as jnp
from jax import lax
from jax.experimental import pallas as pl
from jax.experimental.pallas import tpu as pltpu
from jax.sharding import PartitionSpec as P

coupling = 0.42
mark_rows = 8
f32 = jnp.float32
bf16 = jnp.bfloat16
in_vmem = pl.BlockSpec(memory_space=pltpu.VMEM)
in_smem = pl.BlockSpec(memory_space=pltpu.SMEM)


def send(value, axis, target_of):
    pairs = [(source, target_of(source)) for source in range(lax.axis_size(axis))]
    return lax.ppermute(value, axis, pairs)


def halves(value):
    high = value.astype(bf16)
    return high, (value - high.astype(f32)).astype(bf16)


def dot(left, right):
    return jnp.dot(left, right, preferred_element_type=f32)


def three_pass(left_high, left_low, right):
    high, low = halves(right)
    both = jnp.concatenate([high, low], axis=1)
    order, columns = left_high.shape[0], right.shape[1]
    found = []
    for rows in (slice(0, order // 2), slice(order // 2, order)):
        wide = dot(left_high[rows, :], both)
        found.append(wide[:, :columns] + wide[:, columns:] + dot(left_low[rows, :], high))
    return jnp.concatenate(found, axis=0)


def row_starts(place, shards, width):
    return [pl.multiple_of((place ^ k) * width, width) for k in range(shards)]


def load_rows(ref, starts, width, base=0):
    return jnp.concatenate([ref[pl.ds(base + start, width), :] for start in starts], axis=0)


def store_rows(ref, starts, width, value, base=0):
    for k, start in enumerate(starts):
        ref[pl.ds(base + start, width), :] = value[k * width : (k + 1) * width, :]


def assemble(high, low, refs, starts, width, base=0):
    for k, ref in enumerate(refs):
        for g, start in enumerate(starts):
            at = (slice(g * width, (g + 1) * width), slice(k * width, (k + 1) * width))
            high[at], low[at] = halves(ref[pl.ds(base + start, width), :])


def polynomial(high, low, value):
    second = value + three_pass(high, low, three_pass(high, low, value))
    return second - three_pass(high, low, second)


def compiler_params(megabytes):
    return pltpu.CompilerParams(vmem_limit_bytes=megabytes * 2**20)


def weight(cost):
    return pl.CostEstimate(
        flops=1 + 1_150_000_000 * cost, bytes_accessed=1 + 3_690_000 * cost, transcendentals=0
    )


def kernel_call(body, place, operands, outs, halves_of, after=(), cost=0):
    order = operands[0].shape[1] * lax.axis_size("az")
    width = operands[0].shape[1]
    count = len(operands)
    waited = len(after)

    def kernel(place_ref, *refs):
        starts = row_starts(place_ref[0], order // width, width)
        swapped = pl.multiple_of(place_ref[1] * order, order)
        body(
            starts,
            (swapped, order - swapped),
            refs[:count],
            refs[count + waited : count + waited + len(outs)],
            refs[count + waited + len(outs) :],
        )

    return pl.pallas_call(
        kernel,
        out_shape=[jax.ShapeDtypeStruct((rows, width), f32) for rows in outs],
        in_specs=[in_smem] + [in_vmem] * count + [pl.BlockSpec(memory_space=pl.ANY)] * waited,
        out_specs=[in_vmem] * len(outs),
        scratch_shapes=[pltpu.VMEM((order, order), bf16)] * (2 * halves_of),
        compiler_params=compiler_params(24),
        cost_estimate=weight(cost),
    )(place, *operands, *after)


def couplings(place, lower, upper, after=()):
    order, width = lower.shape

    def body(starts, bases, refs, outs, scratch):
        rows = lax.broadcasted_iota(jnp.int32, (order, width), 0)
        cols = lax.broadcasted_iota(jnp.int32, (order, width), 1)
        diagonal = jnp.where(rows == cols + starts[0], coupling, 0.0)
        outs[0][:order, :] = refs[0][...] - diagonal
        outs[0][order:, :] = refs[1][...] - diagonal

    return kernel_call(body, place, [lower, upper], [2 * order], 0, after)[0]


def normalized(place, n_shards, both, swap=False, join=False, after=()):
    shards, order, width = len(n_shards), both.shape[0] // 2, both.shape[1]

    def body(starts, bases, refs, outs, scratch):
        assemble(*scratch, refs[:shards], starts, width)
        bases = bases if swap else (0, order)
        value = [load_rows(refs[shards], starts, width, base) for base in bases]
        result = polynomial(*scratch, jnp.concatenate(value, axis=1))
        places = ((outs[0], 0), (outs[0], order)) if join else ((outs[0], 0), (outs[1], 0))
        for k, (ref, base) in enumerate(places):
            store_rows(ref, starts, width, result[:, k * width : (k + 1) * width], base)

    return kernel_call(body, place, [*n_shards, both], [2 * order] if join else [order] * 2, 1, after)


def joined_column(place, n_shards, value, one, two, after=()):
    shards, order, width = len(n_shards), *value.shape

    def body(starts, bases, refs, outs, scratch):
        assemble(*scratch, refs[:shards], starts, width)
        result = polynomial(*scratch, load_rows(refs[shards], starts, width))
        for out, top in zip(outs, refs[shards + 1 :]):
            out[:order, :] = top[...]
            store_rows(out, starts, width, result, order)

    return kernel_call(body, place, [*n_shards, value, one, two], [2 * order] * 2, 1, after)


def one_column(place, n_shards, value, after=()):
    shards, order, width = len(n_shards), *value.shape

    def body(starts, bases, refs, outs, scratch):
        assemble(*scratch, refs[:shards], starts, width)
        result = polynomial(*scratch, load_rows(refs[shards], starts, width))
        store_rows(outs[0], starts, width, result)

    return kernel_call(body, place, [*n_shards, value], [order], 1, after)[0]


def advanced(place, both_shards, n_shards, base, one, two, join, after=()):
    shards, order, width = len(both_shards), *base.shape

    def body(starts, bases, refs, outs, scratch):
        total = load_rows(refs[2 * shards], starts, width)
        value = []
        for m in range(2):
            assemble(*scratch[2 * m : 2 * m + 2], refs[:shards], starts, width, m * order)
            right = [load_rows(refs[2 * shards + 1 + m], starts, width, at) for at in (0, order)]
            found = three_pass(*scratch[2 * m : 2 * m + 2], jnp.concatenate(right, axis=1))
            store_rows(outs[0], starts, width, -found[:, :width], m * order)
            value.append(-found[:, :width])
            total = total - found[:, width:]
        store_rows(outs[1], starts, width, total)
        assemble(*scratch[4:], refs[shards : 2 * shards], starts, width)
        result = polynomial(*scratch[4:], jnp.concatenate(value, axis=1))
        places = ((outs[2], 0), (outs[2], order)) if join else ((outs[2], 0), (outs[3], 0))
        for k, (ref, at) in enumerate(places):
            store_rows(ref, starts, width, result[:, k * width : (k + 1) * width], at)

    operands = [*both_shards, *n_shards, base, one, two]
    outs = [2 * order, order] + ([2 * order] if join else [order] * 2)
    return kernel_call(body, place, operands, outs, 3, after)


def reduced(place, both_shards, base, one, two, swap=False, after=(), cost=0):
    shards, order, width = len(both_shards), *base.shape
    joined = one is two

    def body(starts, bases, refs, outs, scratch):
        bases = bases if swap else (0, order)
        total = load_rows(refs[shards], starts, width)
        if joined and one.shape[0] == 2 * order:
            rights = [load_rows(refs[shards + 1], starts, width, at) for at in (order, 0)]
        else:
            rights = [load_rows(ref, starts, width) for ref in refs[shards + 1 :]]
            rights = rights * 2 if joined else rights
        for m in range(2):
            assemble(*scratch[2 * m : 2 * m + 2], refs[:shards], starts, width, bases[m])
            total = total - three_pass(*scratch[2 * m : 2 * m + 2], rights[m])
        store_rows(outs[0], starts, width, total)

    operands = [*both_shards, base, one] if joined else [*both_shards, base, one, two]
    return kernel_call(body, place, operands, [order], 2, after, cost)[0]


def coupled(place, both_shards, one, two, swap=False, after=()):
    shards, order, width = len(both_shards), *one.shape

    def body(starts, bases, refs, outs, scratch):
        bases = bases if swap else (0, order)
        for m in range(2):
            assemble(*scratch[2 * m : 2 * m + 2], refs[:shards], starts, width, bases[m])
            found = three_pass(*scratch[2 * m : 2 * m + 2], load_rows(refs[shards + m], starts, width))
            store_rows(outs[0], starts, width, -found, bases[m])

    return kernel_call(body, place, [*both_shards, one, two], [2 * order], 2, after)[0]


def slots_kernel(cycle_size, slot_count, counts, owner_row, rows_row, extra, out):
    entries, width = extra.shape
    position = lax.broadcasted_iota(jnp.int32, (1, entries), 1)
    live = position < counts[0]
    target = jnp.where(live, owner_row[...], cycle_size)
    blocks = lax.broadcasted_iota(jnp.int32, (cycle_size, entries), 0)
    owned = (blocks == target).astype(f32)
    before = lax.broadcasted_iota(jnp.int32, (entries, entries), 0)
    after = lax.broadcasted_iota(jnp.int32, (entries, entries), 1)
    earlier = dot(owned.astype(bf16), (before < after).astype(f32).astype(bf16))
    rank = jnp.sum(owned * earlier, axis=0, keepdims=True).astype(jnp.int32)
    high, low = halves(extra[...])
    both = jnp.concatenate([high, low], axis=1)
    slots = lax.broadcasted_iota(jnp.int32, (slot_count, entries), 0)
    in_slot = (slots == rank).astype(f32)
    mark_high, mark_low = halves(owned * (rows_row[...] + 1).astype(f32))
    to_slot = lambda mark: lax.dot_general(
        mark, in_slot.astype(bf16), (((1,), (1,)), ((), ())), preferred_element_type=f32
    )
    marks = to_slot(mark_high) + to_slot(mark_low)
    stride = slot_count + mark_rows
    for block in range(cycle_size):
        base = block * stride
        chosen = jnp.where(target == block, in_slot, 0.0).astype(bf16)
        found = dot(chosen, both)
        out[base : base + slot_count, :] = found[:, :width] + found[:, width:]
        out[base + slot_count : base + stride, :] = jnp.zeros((mark_rows, width), f32)
        out[base + slot_count : base + slot_count + 1, :slot_count] = marks[block : block + 1, :]


def load_kernel(cycle_size, slot_count, right_side, got, _, out):
    order, width = right_side.shape
    stride = slot_count + mark_rows
    total = right_side[...]
    rows = (lax.broadcasted_iota(jnp.int32, (order, slot_count), 0) + 1).astype(f32)
    for block in range(cycle_size):
        high, low = halves(got[block * stride : block * stride + slot_count, :])
        marks = got[block * stride + slot_count : block * stride + slot_count + 1, :slot_count]
        chosen = (rows == marks).astype(f32).astype(bf16)
        found = dot(chosen, jnp.concatenate([high, low], axis=1))
        total = total + (found[:, :width] + found[:, width:])
    out[...] = total


def placed_entries(extra, owners, rows_in, counts):
    cycle_size = lax.axis_size("blk")
    entries, width = extra.shape
    slot_count = 2 * entries // cycle_size
    rows = cycle_size * (slot_count + mark_rows)
    return pl.pallas_call(
        functools.partial(slots_kernel, cycle_size, slot_count),
        out_shape=jax.ShapeDtypeStruct((rows, width), f32),
        in_specs=[in_smem] + [in_vmem] * 3,
        out_specs=in_vmem,
        compiler_params=compiler_params(24),
        cost_estimate=weight(0),
    )(counts, owners.reshape(1, entries), rows_in.reshape(1, entries), extra)


def loaded(right_side, got, after):
    cycle_size = lax.axis_size("blk")
    order, width = right_side.shape
    return pl.pallas_call(
        functools.partial(load_kernel, cycle_size, got.shape[1] - mark_rows),
        out_shape=jax.ShapeDtypeStruct((order, width), f32),
        in_specs=[in_vmem] * 2 + [pl.BlockSpec(memory_space=pl.ANY)],
        out_specs=in_vmem,
        compiler_params=compiler_params(24),
        cost_estimate=weight(0),
    )(right_side, got.reshape(-1, width), after)


def across(value):
    bit = lax.axis_size("az") // 2
    return {bit: send(value, "az", lambda source: source ^ bit)}


def gathered(value, far):
    shards = {0: value, **far}
    bit = max(far) // 2
    while bit:
        for k in list(shards):
            shards[k | bit] = send(shards[k], "az", lambda source, bit=bit: source ^ bit)
        bit //= 2
    return [shards[k] for k in range(len(shards))]


def tied(*values):
    return lax.optimization_barrier(values)


def on_device(lower_part, diag_part, upper_part, right_side, extra, owners, rows_in, counts):
    cycle_size = lax.axis_size("blk")
    levels = min(4, 3 + cycle_size // 16)
    blk = lax.axis_index("blk")
    place = jnp.stack([lax.axis_index("az"), blk % 2]).astype(jnp.int32)
    diag = diag_part[0]

    n_far = across(diag)
    slots = placed_entries(extra, owners, rows_in, counts)
    both = couplings(place, lower_part[0], upper_part[0], [slots])
    n_far, both = tied(n_far, both)
    n_shards = gathered(diag, n_far)

    partner = lambda source: source ^ 1
    onward = lambda source: (source + 2 - 4 * (source % 2)) % cycle_size
    got_slots = lax.all_to_all(
        slots.reshape(cycle_size, -1, slots.shape[1]), "blk", split_axis=0, concat_axis=0, tiled=True
    )
    first, second = normalized(place, n_shards, both, swap=True)
    both_shards = gathered(both, across(both))
    near_first = send(first, "blk", partner)
    near_second = send(second, "blk", partner)
    near_first, got_slots = tied(near_first, got_slots)
    far_first = send(near_first, "blk", onward)
    right = loaded(right_side[0], got_slots, first)
    solved = one_column(place, n_shards, right)
    near_second, solved = tied(near_second, solved)
    diag = reduced(place, both_shards, diag, far_first, near_second, swap=True, cost=20)
    n_far = across(diag)
    far_second = send(near_second, "blk", onward)
    both = coupled(place, both_shards, far_second, near_first, swap=True, after=[diag])
    near_solved = send(solved, "blk", partner)
    n_far, both = tied(n_far, both)
    n_shards = gathered(diag, n_far)
    far_solved = send(near_solved, "blk", onward)
    right = reduced(place, both_shards, right, far_solved, near_solved, swap=True, cost=20)

    stride = 2
    closing = lambda level, stride: level == levels - 1 and 2 * stride == cycle_size
    pieces = normalized(place, n_shards, both, join=closing(1, stride))
    for level in range(1, levels):
        ahead = lambda source: (source + stride) % cycle_size
        back = lambda source: (source - stride) % cycle_size
        both_far = across(both)
        half = max(both_far)
        if closing(level, stride):
            (pair,) = pieces
            got = send(pair, "blk", ahead)
            both_far[half], late = tied(both_far[half], pair)
            both_shards = gathered(both, both_far)
            solved = one_column(place, n_shards, right, after=[late])
            solved, got = tied(solved, got)
            low_y = send(solved, "blk", ahead)
            diag = reduced(place, both_shards, diag, got, got)
            n_far = across(diag)
            n_far[half], low_y = tied(n_far[half], low_y)
            right = reduced(place, both_shards, right, low_y, low_y, after=[diag], cost=20)
            n_shards = gathered(diag, n_far)
        else:
            p_row, q_row = pieces
            low_q, up_p = send(q_row, "blk", ahead), send(p_row, "blk", back)
            p_solved, q_solved = joined_column(place, n_shards, right, p_row, q_row)
            both_far[half], low_q, up_p, p_solved, q_solved = tied(
                both_far[half], low_q, up_p, p_solved, q_solved
            )
            both_shards = gathered(both, both_far)
            diag = reduced(place, both_shards, diag, low_q, up_p)
            n_shards = gathered(diag, across(diag))
            low, up = send(p_solved, "blk", ahead), send(q_solved, "blk", back)
            both, right, *pieces = advanced(
                place, both_shards, n_shards, right, low, up, closing(level + 1, 2 * stride)
            )
        stride = 2 * stride
    return one_column(place, n_shards, right)[None]


def solution(mesh):
    placed = (
        P("blk", None, "az"),
        P("blk", None, "az"),
        P("blk", None, "az"),
        P("blk", None, "az"),
        P("blk", "az"),
        P("blk", None),
        P("blk"),
        P("blk"),
    )
    return jax.shard_map(
        on_device, mesh=mesh, in_specs=placed, out_specs=P("blk", None, "az"), check_vma=False
    )
```

```python
import functools

import jax
import jax.numpy as jnp
from jax import lax
from jax.experimental import pallas as pl
from jax.experimental.pallas import tpu as pltpu
from jax.sharding import PartitionSpec as P

coupling = 0.42
mark_rows = 8
f32 = jnp.float32
bf16 = jnp.bfloat16
in_vmem = pl.BlockSpec(memory_space=pltpu.VMEM)
in_smem = pl.BlockSpec(memory_space=pltpu.SMEM)


def send(value, axis, target_of):
    pairs = [(source, target_of(source)) for source in range(lax.axis_size(axis))]
    return lax.ppermute(value, axis, pairs)


def halves(value):
    high = value.astype(bf16)
    return high, (value - high.astype(f32)).astype(bf16)


def dot(left, right):
    return jnp.dot(left, right, preferred_element_type=f32)


def three_pass(left_high, left_low, right):
    high, low = halves(right)
    both = jnp.concatenate([high, low], axis=1)
    order, columns = left_high.shape[0], right.shape[1]
    found = []
    for rows in (slice(0, order // 2), slice(order // 2, order)):
        wide = dot(left_high[rows, :], both)
        found.append(wide[:, :columns] + wide[:, columns:] + dot(left_low[rows, :], high))
    return jnp.concatenate(found, axis=0)


def row_starts(place, shards, width):
    return [pl.multiple_of((place ^ k) * width, width) for k in range(shards)]


def load_rows(ref, starts, width, base=0):
    return jnp.concatenate([ref[pl.ds(base + start, width), :] for start in starts], axis=0)


def store_rows(ref, starts, width, value, base=0):
    for k, start in enumerate(starts):
        ref[pl.ds(base + start, width), :] = value[k * width : (k + 1) * width, :]


def assemble(high, low, refs, starts, width, base=0):
    for k, ref in enumerate(refs):
        for g, start in enumerate(starts):
            at = (slice(g * width, (g + 1) * width), slice(k * width, (k + 1) * width))
            high[at], low[at] = halves(ref[pl.ds(base + start, width), :])


def polynomial(high, low, value):
    second = value + three_pass(high, low, three_pass(high, low, value))
    return second - three_pass(high, low, second)


def compiler_params(megabytes):
    return pltpu.CompilerParams(vmem_limit_bytes=megabytes * 2**20)


def weight(cost):
    return pl.CostEstimate(
        flops=1 + 1_150_000_000 * cost, bytes_accessed=1 + 3_690_000 * cost, transcendentals=0
    )


def kernel_call(body, place, operands, outs, halves_of, after=(), cost=0):
    order = operands[0].shape[1] * lax.axis_size("az")
    width = operands[0].shape[1]
    count = len(operands)
    waited = len(after)

    def kernel(place_ref, *refs):
        starts = row_starts(place_ref[0], order // width, width)
        swapped = pl.multiple_of(place_ref[1] * order, order)
        body(
            starts,
            (swapped, order - swapped),
            refs[:count],
            refs[count + waited : count + waited + len(outs)],
            refs[count + waited + len(outs) :],
        )

    return pl.pallas_call(
        kernel,
        out_shape=[jax.ShapeDtypeStruct((rows, width), f32) for rows in outs],
        in_specs=[in_smem] + [in_vmem] * count + [pl.BlockSpec(memory_space=pl.ANY)] * waited,
        out_specs=[in_vmem] * len(outs),
        scratch_shapes=[pltpu.VMEM((order, order), bf16)] * (2 * halves_of),
        compiler_params=compiler_params(24),
        cost_estimate=weight(cost),
    )(place, *operands, *after)


def couplings(place, lower, upper, after=()):
    order, width = lower.shape

    def body(starts, bases, refs, outs, scratch):
        rows = lax.broadcasted_iota(jnp.int32, (order, width), 0)
        cols = lax.broadcasted_iota(jnp.int32, (order, width), 1)
        diagonal = jnp.where(rows == cols + starts[0], coupling, 0.0)
        outs[0][:order, :] = refs[0][...] - diagonal
        outs[0][order:, :] = refs[1][...] - diagonal

    return kernel_call(body, place, [lower, upper], [2 * order], 0, after)[0]


def normalized(place, n_shards, both, swap=False, join=False, after=()):
    shards, order, width = len(n_shards), both.shape[0] // 2, both.shape[1]

    def body(starts, bases, refs, outs, scratch):
        assemble(*scratch, refs[:shards], starts, width)
        bases = bases if swap else (0, order)
        value = [load_rows(refs[shards], starts, width, base) for base in bases]
        result = polynomial(*scratch, jnp.concatenate(value, axis=1))
        places = ((outs[0], 0), (outs[0], order)) if join else ((outs[0], 0), (outs[1], 0))
        for k, (ref, base) in enumerate(places):
            store_rows(ref, starts, width, result[:, k * width : (k + 1) * width], base)

    return kernel_call(body, place, [*n_shards, both], [2 * order] if join else [order] * 2, 1, after)


def joined_column(place, n_shards, value, one, two, after=()):
    shards, order, width = len(n_shards), *value.shape

    def body(starts, bases, refs, outs, scratch):
        assemble(*scratch, refs[:shards], starts, width)
        result = polynomial(*scratch, load_rows(refs[shards], starts, width))
        for out, top in zip(outs, refs[shards + 1 :]):
            out[:order, :] = top[...]
            store_rows(out, starts, width, result, order)

    return kernel_call(body, place, [*n_shards, value, one, two], [2 * order] * 2, 1, after)


def one_column(place, n_shards, value, after=()):
    shards, order, width = len(n_shards), *value.shape

    def body(starts, bases, refs, outs, scratch):
        assemble(*scratch, refs[:shards], starts, width)
        result = polynomial(*scratch, load_rows(refs[shards], starts, width))
        store_rows(outs[0], starts, width, result)

    return kernel_call(body, place, [*n_shards, value], [order], 1, after)[0]


def advanced(place, both_shards, n_shards, base, one, two, join, after=()):
    shards, order, width = len(both_shards), *base.shape

    def body(starts, bases, refs, outs, scratch):
        total = load_rows(refs[2 * shards], starts, width)
        value = []
        for m in range(2):
            assemble(*scratch[2 * m : 2 * m + 2], refs[:shards], starts, width, m * order)
            right = [load_rows(refs[2 * shards + 1 + m], starts, width, at) for at in (0, order)]
            found = three_pass(*scratch[2 * m : 2 * m + 2], jnp.concatenate(right, axis=1))
            store_rows(outs[0], starts, width, -found[:, :width], m * order)
            value.append(-found[:, :width])
            total = total - found[:, width:]
        store_rows(outs[1], starts, width, total)
        assemble(*scratch[4:], refs[shards : 2 * shards], starts, width)
        result = polynomial(*scratch[4:], jnp.concatenate(value, axis=1))
        places = ((outs[2], 0), (outs[2], order)) if join else ((outs[2], 0), (outs[3], 0))
        for k, (ref, at) in enumerate(places):
            store_rows(ref, starts, width, result[:, k * width : (k + 1) * width], at)

    operands = [*both_shards, *n_shards, base, one, two]
    outs = [2 * order, order] + ([2 * order] if join else [order] * 2)
    return kernel_call(body, place, operands, outs, 3, after)


def reduced(place, both_shards, base, one, two, swap=False, after=(), cost=0):
    shards, order, width = len(both_shards), *base.shape
    joined = one is two

    def body(starts, bases, refs, outs, scratch):
        bases = bases if swap else (0, order)
        total = load_rows(refs[shards], starts, width)
        if joined and one.shape[0] == 2 * order:
            rights = [load_rows(refs[shards + 1], starts, width, at) for at in (order, 0)]
        else:
            rights = [load_rows(ref, starts, width) for ref in refs[shards + 1 :]]
            rights = rights * 2 if joined else rights
        for m in range(2):
            assemble(*scratch[2 * m : 2 * m + 2], refs[:shards], starts, width, bases[m])
            total = total - three_pass(*scratch[2 * m : 2 * m + 2], rights[m])
        store_rows(outs[0], starts, width, total)

    operands = [*both_shards, base, one] if joined else [*both_shards, base, one, two]
    return kernel_call(body, place, operands, [order], 2, after, cost)[0]


def coupled(place, both_shards, one, two, swap=False, after=()):
    shards, order, width = len(both_shards), *one.shape

    def body(starts, bases, refs, outs, scratch):
        bases = bases if swap else (0, order)
        for m in range(2):
            assemble(*scratch[2 * m : 2 * m + 2], refs[:shards], starts, width, bases[m])
            found = three_pass(*scratch[2 * m : 2 * m + 2], load_rows(refs[shards + m], starts, width))
            store_rows(outs[0], starts, width, -found, bases[m])

    return kernel_call(body, place, [*both_shards, one, two], [2 * order], 2, after)[0]


def slots_kernel(cycle_size, slot_count, counts, owner_row, rows_row, extra, out):
    entries, width = extra.shape
    position = lax.broadcasted_iota(jnp.int32, (1, entries), 1)
    live = position < counts[0]
    target = jnp.where(live, owner_row[...], cycle_size)
    blocks = lax.broadcasted_iota(jnp.int32, (cycle_size, entries), 0)
    owned = (blocks == target).astype(f32)
    before = lax.broadcasted_iota(jnp.int32, (entries, entries), 0)
    after = lax.broadcasted_iota(jnp.int32, (entries, entries), 1)
    earlier = dot(owned.astype(bf16), (before < after).astype(f32).astype(bf16))
    rank = jnp.sum(owned * earlier, axis=0, keepdims=True).astype(jnp.int32)
    high, low = halves(extra[...])
    both = jnp.concatenate([high, low], axis=1)
    slots = lax.broadcasted_iota(jnp.int32, (slot_count, entries), 0)
    in_slot = (slots == rank).astype(f32)
    mark_high, mark_low = halves(owned * (rows_row[...] + 1).astype(f32))
    to_slot = lambda mark: lax.dot_general(
        mark, in_slot.astype(bf16), (((1,), (1,)), ((), ())), preferred_element_type=f32
    )
    marks = to_slot(mark_high) + to_slot(mark_low)
    stride = slot_count + mark_rows
    for block in range(cycle_size):
        base = block * stride
        chosen = jnp.where(target == block, in_slot, 0.0).astype(bf16)
        found = dot(chosen, both)
        out[base : base + slot_count, :] = found[:, :width] + found[:, width:]
        out[base + slot_count : base + stride, :] = jnp.zeros((mark_rows, width), f32)
        out[base + slot_count : base + slot_count + 1, :slot_count] = marks[block : block + 1, :]


def load_kernel(cycle_size, slot_count, right_side, got, _, out):
    order, width = right_side.shape
    stride = slot_count + mark_rows
    total = right_side[...]
    rows = (lax.broadcasted_iota(jnp.int32, (order, slot_count), 0) + 1).astype(f32)
    for block in range(cycle_size):
        high, low = halves(got[block * stride : block * stride + slot_count, :])
        marks = got[block * stride + slot_count : block * stride + slot_count + 1, :slot_count]
        chosen = (rows == marks).astype(f32).astype(bf16)
        found = dot(chosen, jnp.concatenate([high, low], axis=1))
        total = total + (found[:, :width] + found[:, width:])
    out[...] = total


def placed_entries(extra, owners, rows_in, counts):
    cycle_size = lax.axis_size("blk")
    entries, width = extra.shape
    slot_count = 2 * entries // cycle_size
    rows = cycle_size * (slot_count + mark_rows)
    return pl.pallas_call(
        functools.partial(slots_kernel, cycle_size, slot_count),
        out_shape=jax.ShapeDtypeStruct((rows, width), f32),
        in_specs=[in_smem] + [in_vmem] * 3,
        out_specs=in_vmem,
        compiler_params=compiler_params(24),
        cost_estimate=weight(0),
    )(counts, owners.reshape(1, entries), rows_in.reshape(1, entries), extra)


def loaded(right_side, got, after):
    cycle_size = lax.axis_size("blk")
    order, width = right_side.shape
    return pl.pallas_call(
        functools.partial(load_kernel, cycle_size, got.shape[1] - mark_rows),
        out_shape=jax.ShapeDtypeStruct((order, width), f32),
        in_specs=[in_vmem] * 2 + [pl.BlockSpec(memory_space=pl.ANY)],
        out_specs=in_vmem,
        compiler_params=compiler_params(24),
        cost_estimate=weight(0),
    )(right_side, got.reshape(-1, width), after)


def across(value):
    bit = lax.axis_size("az") // 2
    return {bit: send(value, "az", lambda source: source ^ bit)}


def gathered(value, far):
    shards = {0: value, **far}
    bit = max(far) // 2
    while bit:
        for k in list(shards):
            shards[k | bit] = send(shards[k], "az", lambda source, bit=bit: source ^ bit)
        bit //= 2
    return [shards[k] for k in range(len(shards))]


def tied(*values):
    return lax.optimization_barrier(values)


def on_device(lower_part, diag_part, upper_part, right_side, extra, owners, rows_in, counts):
    cycle_size = lax.axis_size("blk")
    levels = min(4, 3 + cycle_size // 16)
    blk = lax.axis_index("blk")
    place = jnp.stack([lax.axis_index("az"), blk % 2]).astype(jnp.int32)
    diag = diag_part[0]

    n_far = across(diag)
    slots = placed_entries(extra, owners, rows_in, counts)
    both = couplings(place, lower_part[0], upper_part[0], [slots, *n_far.values()])
    n_shards = gathered(diag, n_far)

    partner = lambda source: source ^ 1
    onward = lambda source: (source + 2 - 4 * (source % 2)) % cycle_size
    got_slots = lax.all_to_all(
        slots.reshape(cycle_size, -1, slots.shape[1]), "blk", split_axis=0, concat_axis=0, tiled=True
    )
    first, second = normalized(place, n_shards, both, swap=True)
    both_shards = gathered(both, across(both))
    near_first = send(first, "blk", partner)
    near_second = send(second, "blk", partner)
    near_first, got_slots = tied(near_first, got_slots)
    far_first = send(near_first, "blk", onward)
    right = loaded(right_side[0], got_slots, first)
    solved = one_column(place, n_shards, right)
    near_second, solved = tied(near_second, solved)
    diag = reduced(place, both_shards, diag, far_first, near_second, swap=True, cost=20)
    n_far = across(diag)
    far_second = send(near_second, "blk", onward)
    both = coupled(place, both_shards, far_second, near_first, swap=True, after=[diag])
    near_solved = send(solved, "blk", partner)
    n_far, both = tied(n_far, both)
    n_shards = gathered(diag, n_far)
    far_solved = send(near_solved, "blk", onward)
    right = reduced(place, both_shards, right, far_solved, near_solved, swap=True, cost=20)

    stride = 2
    closing = lambda level, stride: level == levels - 1 and 2 * stride == cycle_size
    pieces = normalized(place, n_shards, both, join=closing(1, stride))
    for level in range(1, levels):
        ahead = lambda source: (source + stride) % cycle_size
        back = lambda source: (source - stride) % cycle_size
        both_far = across(both)
        half = max(both_far)
        if closing(level, stride):
            (pair,) = pieces
            got = send(pair, "blk", ahead)
            solved = one_column(place, n_shards, right, after=[pair])
            both_far[half], got, solved = tied(both_far[half], got, solved)
            both_shards = gathered(both, both_far)
            low_y = send(solved, "blk", ahead)
            diag = reduced(place, both_shards, diag, got, got)
            n_far = across(diag)
            n_far[half], low_y = tied(n_far[half], low_y)
            right = reduced(place, both_shards, right, low_y, low_y, after=[diag], cost=20)
            n_shards = gathered(diag, n_far)
        else:
            p_row, q_row = pieces
            low_q, up_p = send(q_row, "blk", ahead), send(p_row, "blk", back)
            p_solved, q_solved = joined_column(place, n_shards, right, p_row, q_row)
            both_far[half], low_q, up_p, p_solved, q_solved = tied(
                both_far[half], low_q, up_p, p_solved, q_solved
            )
            both_shards = gathered(both, both_far)
            diag = reduced(place, both_shards, diag, low_q, up_p)
            n_shards = gathered(diag, across(diag))
            low, up = send(p_solved, "blk", ahead), send(q_solved, "blk", back)
            both, right, *pieces = advanced(
                place, both_shards, n_shards, right, low, up, closing(level + 1, 2 * stride)
            )
        stride = 2 * stride
    return one_column(place, n_shards, right)[None]


def solution(mesh):
    placed = (
        P("blk", None, "az"),
        P("blk", None, "az"),
        P("blk", None, "az"),
        P("blk", None, "az"),
        P("blk", "az"),
        P("blk", None),
        P("blk"),
        P("blk"),
    )
    return jax.shard_map(
        on_device, mesh=mesh, in_specs=placed, out_specs=P("blk", None, "az"), check_vma=False
    )
```

```python
import functools

import jax
import jax.numpy as jnp
from jax import lax
from jax.experimental import pallas as pl
from jax.experimental.pallas import tpu as pltpu
from jax.sharding import PartitionSpec as P

coupling = 0.42
mark_rows = 8
f32 = jnp.float32
bf16 = jnp.bfloat16
in_vmem = pl.BlockSpec(memory_space=pltpu.VMEM)
in_smem = pl.BlockSpec(memory_space=pltpu.SMEM)


def send(value, axis, target_of):
    pairs = [(source, target_of(source)) for source in range(lax.axis_size(axis))]
    return lax.ppermute(value, axis, pairs)


def halves(value):
    high = value.astype(bf16)
    return high, (value - high.astype(f32)).astype(bf16)


def dot(left, right):
    return jnp.dot(left, right, preferred_element_type=f32)


def three_pass(left_high, left_low, right):
    high, low = halves(right)
    both = jnp.concatenate([high, low], axis=1)
    order, columns = left_high.shape[0], right.shape[1]
    found = []
    for rows in (slice(0, order // 2), slice(order // 2, order)):
        wide = dot(left_high[rows, :], both)
        found.append(wide[:, :columns] + wide[:, columns:] + dot(left_low[rows, :], high))
    return jnp.concatenate(found, axis=0)


def row_starts(place, shards, width):
    return [pl.multiple_of((place ^ k) * width, width) for k in range(shards)]


def load_rows(ref, starts, width, base=0):
    return jnp.concatenate([ref[pl.ds(base + start, width), :] for start in starts], axis=0)


def store_rows(ref, starts, width, value, base=0):
    for k, start in enumerate(starts):
        ref[pl.ds(base + start, width), :] = value[k * width : (k + 1) * width, :]


def assemble(high, low, refs, starts, width, base=0):
    for k, ref in enumerate(refs):
        for g, start in enumerate(starts):
            at = (slice(g * width, (g + 1) * width), slice(k * width, (k + 1) * width))
            high[at], low[at] = halves(ref[pl.ds(base + start, width), :])


def polynomial(high, low, value):
    second = value + three_pass(high, low, three_pass(high, low, value))
    return second - three_pass(high, low, second)


def compiler_params(megabytes):
    return pltpu.CompilerParams(vmem_limit_bytes=megabytes * 2**20)


def weight(cost):
    return pl.CostEstimate(
        flops=1 + 1_150_000_000 * cost, bytes_accessed=1 + 3_690_000 * cost, transcendentals=0
    )


def kernel_call(body, place, operands, outs, halves_of, after=(), cost=0):
    order = operands[0].shape[1] * lax.axis_size("az")
    width = operands[0].shape[1]
    count = len(operands)
    waited = len(after)

    def kernel(place_ref, *refs):
        starts = row_starts(place_ref[0], order // width, width)
        swapped = pl.multiple_of(place_ref[1] * order, order)
        body(
            starts,
            (swapped, order - swapped),
            refs[:count],
            refs[count + waited : count + waited + len(outs)],
            refs[count + waited + len(outs) :],
        )

    return pl.pallas_call(
        kernel,
        out_shape=[jax.ShapeDtypeStruct((rows, width), f32) for rows in outs],
        in_specs=[in_smem] + [in_vmem] * count + [pl.BlockSpec(memory_space=pl.ANY)] * waited,
        out_specs=[in_vmem] * len(outs),
        scratch_shapes=[pltpu.VMEM((order, order), bf16)] * (2 * halves_of),
        compiler_params=compiler_params(24),
        cost_estimate=weight(cost),
    )(place, *operands, *after)


def couplings(place, lower, upper, after=()):
    order, width = lower.shape

    def body(starts, bases, refs, outs, scratch):
        rows = lax.broadcasted_iota(jnp.int32, (order, width), 0)
        cols = lax.broadcasted_iota(jnp.int32, (order, width), 1)
        diagonal = jnp.where(rows == cols + starts[0], coupling, 0.0)
        outs[0][:order, :] = refs[0][...] - diagonal
        outs[0][order:, :] = refs[1][...] - diagonal

    return kernel_call(body, place, [lower, upper], [2 * order], 0, after)[0]


def normalized(place, n_shards, both, swap=False, join=False, after=()):
    shards, order, width = len(n_shards), both.shape[0] // 2, both.shape[1]

    def body(starts, bases, refs, outs, scratch):
        assemble(*scratch, refs[:shards], starts, width)
        bases = bases if swap else (0, order)
        value = [load_rows(refs[shards], starts, width, base) for base in bases]
        result = polynomial(*scratch, jnp.concatenate(value, axis=1))
        places = ((outs[0], 0), (outs[0], order)) if join else ((outs[0], 0), (outs[1], 0))
        for k, (ref, base) in enumerate(places):
            store_rows(ref, starts, width, result[:, k * width : (k + 1) * width], base)

    return kernel_call(body, place, [*n_shards, both], [2 * order] if join else [order] * 2, 1, after)


def joined_column(place, n_shards, value, one, two, after=()):
    shards, order, width = len(n_shards), *value.shape

    def body(starts, bases, refs, outs, scratch):
        assemble(*scratch, refs[:shards], starts, width)
        result = polynomial(*scratch, load_rows(refs[shards], starts, width))
        for out, top in zip(outs, refs[shards + 1 :]):
            out[:order, :] = top[...]
            store_rows(out, starts, width, result, order)

    return kernel_call(body, place, [*n_shards, value, one, two], [2 * order] * 2, 1, after)


def one_column(place, n_shards, value, after=()):
    shards, order, width = len(n_shards), *value.shape

    def body(starts, bases, refs, outs, scratch):
        assemble(*scratch, refs[:shards], starts, width)
        result = polynomial(*scratch, load_rows(refs[shards], starts, width))
        store_rows(outs[0], starts, width, result)

    return kernel_call(body, place, [*n_shards, value], [order], 1, after)[0]


def advanced(place, both_shards, n_shards, base, one, two, join, after=()):
    shards, order, width = len(both_shards), *base.shape

    def body(starts, bases, refs, outs, scratch):
        total = load_rows(refs[2 * shards], starts, width)
        value = []
        for m in range(2):
            assemble(*scratch[2 * m : 2 * m + 2], refs[:shards], starts, width, m * order)
            right = [load_rows(refs[2 * shards + 1 + m], starts, width, at) for at in (0, order)]
            found = three_pass(*scratch[2 * m : 2 * m + 2], jnp.concatenate(right, axis=1))
            store_rows(outs[0], starts, width, -found[:, :width], m * order)
            value.append(-found[:, :width])
            total = total - found[:, width:]
        store_rows(outs[1], starts, width, total)
        assemble(*scratch[4:], refs[shards : 2 * shards], starts, width)
        result = polynomial(*scratch[4:], jnp.concatenate(value, axis=1))
        places = ((outs[2], 0), (outs[2], order)) if join else ((outs[2], 0), (outs[3], 0))
        for k, (ref, at) in enumerate(places):
            store_rows(ref, starts, width, result[:, k * width : (k + 1) * width], at)

    operands = [*both_shards, *n_shards, base, one, two]
    outs = [2 * order, order] + ([2 * order] if join else [order] * 2)
    return kernel_call(body, place, operands, outs, 3, after)


def reduced(place, both_shards, base, one, two, swap=False, after=(), cost=0):
    shards, order, width = len(both_shards), *base.shape
    joined = one is two

    def body(starts, bases, refs, outs, scratch):
        bases = bases if swap else (0, order)
        total = load_rows(refs[shards], starts, width)
        if joined and one.shape[0] == 2 * order:
            rights = [load_rows(refs[shards + 1], starts, width, at) for at in (order, 0)]
        else:
            rights = [load_rows(ref, starts, width) for ref in refs[shards + 1 :]]
            rights = rights * 2 if joined else rights
        for m in range(2):
            assemble(*scratch[2 * m : 2 * m + 2], refs[:shards], starts, width, bases[m])
            total = total - three_pass(*scratch[2 * m : 2 * m + 2], rights[m])
        store_rows(outs[0], starts, width, total)

    operands = [*both_shards, base, one] if joined else [*both_shards, base, one, two]
    return kernel_call(body, place, operands, [order], 2, after, cost)[0]


def coupled(place, both_shards, one, two, swap=False, after=()):
    shards, order, width = len(both_shards), *one.shape

    def body(starts, bases, refs, outs, scratch):
        bases = bases if swap else (0, order)
        for m in range(2):
            assemble(*scratch[2 * m : 2 * m + 2], refs[:shards], starts, width, bases[m])
            found = three_pass(*scratch[2 * m : 2 * m + 2], load_rows(refs[shards + m], starts, width))
            store_rows(outs[0], starts, width, -found, bases[m])

    return kernel_call(body, place, [*both_shards, one, two], [2 * order], 2, after)[0]


def slots_kernel(cycle_size, slot_count, counts, names, extra, out):
    entries, width = extra.shape
    position = lax.broadcasted_iota(jnp.int32, (1, entries), 1)
    live = position < counts[0]
    target = jnp.where(live, names[:1, :], cycle_size)
    blocks = lax.broadcasted_iota(jnp.int32, (cycle_size, entries), 0)
    owned = (blocks == target).astype(f32)
    before = lax.broadcasted_iota(jnp.int32, (entries, entries), 0)
    after = lax.broadcasted_iota(jnp.int32, (entries, entries), 1)
    earlier = dot(owned.astype(bf16), (before < after).astype(f32).astype(bf16))
    rank = jnp.sum(owned * earlier, axis=0, keepdims=True).astype(jnp.int32)
    high, low = halves(extra[...])
    both = jnp.concatenate([high, low], axis=1)
    slots = lax.broadcasted_iota(jnp.int32, (slot_count, entries), 0)
    in_slot = (slots == rank).astype(f32)
    mark_high, mark_low = halves(owned * (names[1:2, :] + 1).astype(f32))
    to_slot = lambda mark: lax.dot_general(
        mark, in_slot.astype(bf16), (((1,), (1,)), ((), ())), preferred_element_type=f32
    )
    marks = to_slot(mark_high) + to_slot(mark_low)
    stride = slot_count + mark_rows
    for block in range(cycle_size):
        base = block * stride
        chosen = jnp.where(target == block, in_slot, 0.0).astype(bf16)
        found = dot(chosen, both)
        out[base : base + slot_count, :] = found[:, :width] + found[:, width:]
        out[base + slot_count : base + stride, :] = jnp.zeros((mark_rows, width), f32)
        out[base + slot_count : base + slot_count + 1, :slot_count] = marks[block : block + 1, :]


def load_kernel(cycle_size, slot_count, right_side, got, _, out):
    order, width = right_side.shape
    stride = slot_count + mark_rows
    total = right_side[...]
    rows = (lax.broadcasted_iota(jnp.int32, (order, slot_count), 0) + 1).astype(f32)
    for block in range(cycle_size):
        high, low = halves(got[block * stride : block * stride + slot_count, :])
        marks = got[block * stride + slot_count : block * stride + slot_count + 1, :slot_count]
        chosen = (rows == marks).astype(f32).astype(bf16)
        found = dot(chosen, jnp.concatenate([high, low], axis=1))
        total = total + (found[:, :width] + found[:, width:])
    out[...] = total


def placed_entries(extra, owners, rows_in, counts):
    cycle_size = lax.axis_size("blk")
    entries, width = extra.shape
    slot_count = 2 * entries // cycle_size
    rows = cycle_size * (slot_count + mark_rows)
    names = jnp.concatenate([owners.reshape(1, entries), rows_in.reshape(1, entries)], axis=0)
    return pl.pallas_call(
        functools.partial(slots_kernel, cycle_size, slot_count),
        out_shape=jax.ShapeDtypeStruct((rows, width), f32),
        in_specs=[in_smem] + [in_vmem] * 2,
        out_specs=in_vmem,
        compiler_params=compiler_params(24),
        cost_estimate=weight(0),
    )(counts, names, extra)


def loaded(right_side, got, after):
    cycle_size = lax.axis_size("blk")
    order, width = right_side.shape
    return pl.pallas_call(
        functools.partial(load_kernel, cycle_size, got.shape[1] - mark_rows),
        out_shape=jax.ShapeDtypeStruct((order, width), f32),
        in_specs=[in_vmem] * 2 + [pl.BlockSpec(memory_space=pl.ANY)],
        out_specs=in_vmem,
        compiler_params=compiler_params(24),
        cost_estimate=weight(0),
    )(right_side, got.reshape(-1, width), after)


def across(value):
    bit = lax.axis_size("az") // 2
    return {bit: send(value, "az", lambda source: source ^ bit)}


def gathered(value, far):
    shards = {0: value, **far}
    bit = max(far) // 2
    while bit:
        for k in list(shards):
            shards[k | bit] = send(shards[k], "az", lambda source, bit=bit: source ^ bit)
        bit //= 2
    return [shards[k] for k in range(len(shards))]


def tied(*values):
    return lax.optimization_barrier(values)


def on_device(lower_part, diag_part, upper_part, right_side, extra, owners, rows_in, counts):
    cycle_size = lax.axis_size("blk")
    levels = min(4, 3 + cycle_size // 16)
    blk = lax.axis_index("blk")
    place = jnp.stack([lax.axis_index("az"), blk % 2]).astype(jnp.int32)
    diag = diag_part[0]

    n_far = across(diag)
    slots = placed_entries(extra, owners, rows_in, counts)
    both = couplings(place, lower_part[0], upper_part[0], [slots, *n_far.values()])
    n_shards = gathered(diag, n_far)

    partner = lambda source: source ^ 1
    onward = lambda source: (source + 2 - 4 * (source % 2)) % cycle_size
    got_slots = lax.all_to_all(
        slots.reshape(cycle_size, -1, slots.shape[1]), "blk", split_axis=0, concat_axis=0, tiled=True
    )
    first, second = normalized(place, n_shards, both, swap=True)
    both_shards = gathered(both, across(both))
    near_first = send(first, "blk", partner)
    near_second = send(second, "blk", partner)
    near_first, got_slots = tied(near_first, got_slots)
    far_first = send(near_first, "blk", onward)
    right = loaded(right_side[0], got_slots, first)
    solved = one_column(place, n_shards, right)
    near_second, solved = tied(near_second, solved)
    diag = reduced(place, both_shards, diag, far_first, near_second, swap=True, cost=20)
    n_far = across(diag)
    far_second = send(near_second, "blk", onward)
    both = coupled(place, both_shards, far_second, near_first, swap=True, after=[diag])
    near_solved = send(solved, "blk", partner)
    n_far, both = tied(n_far, both)
    n_shards = gathered(diag, n_far)
    far_solved = send(near_solved, "blk", onward)
    right = reduced(place, both_shards, right, far_solved, near_solved, swap=True, cost=20)

    stride = 2
    closing = lambda level, stride: level == levels - 1 and 2 * stride == cycle_size
    pieces = normalized(place, n_shards, both, join=closing(1, stride))
    for level in range(1, levels):
        ahead = lambda source: (source + stride) % cycle_size
        back = lambda source: (source - stride) % cycle_size
        both_far = across(both)
        half = max(both_far)
        if closing(level, stride):
            (pair,) = pieces
            got = send(pair, "blk", ahead)
            solved = one_column(place, n_shards, right, after=[pair])
            both_far[half], got, solved = tied(both_far[half], got, solved)
            both_shards = gathered(both, both_far)
            low_y = send(solved, "blk", ahead)
            diag = reduced(place, both_shards, diag, got, got)
            n_far = across(diag)
            n_far[half], low_y = tied(n_far[half], low_y)
            right = reduced(place, both_shards, right, low_y, low_y, after=[diag], cost=20)
            n_shards = gathered(diag, n_far)
        else:
            p_row, q_row = pieces
            low_q, up_p = send(q_row, "blk", ahead), send(p_row, "blk", back)
            p_solved, q_solved = joined_column(place, n_shards, right, p_row, q_row)
            both_far[half], low_q, up_p, p_solved, q_solved = tied(
                both_far[half], low_q, up_p, p_solved, q_solved
            )
            both_shards = gathered(both, both_far)
            diag = reduced(place, both_shards, diag, low_q, up_p)
            n_shards = gathered(diag, across(diag))
            low, up = send(p_solved, "blk", ahead), send(q_solved, "blk", back)
            both, right, *pieces = advanced(
                place, both_shards, n_shards, right, low, up, closing(level + 1, 2 * stride)
            )
        stride = 2 * stride
    return one_column(place, n_shards, right)[None]


def solution(mesh):
    placed = (
        P("blk", None, "az"),
        P("blk", None, "az"),
        P("blk", None, "az"),
        P("blk", None, "az"),
        P("blk", "az"),
        P("blk", None),
        P("blk"),
        P("blk"),
    )
    return jax.shard_map(
        on_device, mesh=mesh, in_specs=placed, out_specs=P("blk", None, "az"), check_vma=False
    )
```
